32 devices in a mesh: ctx: 32 (over z, y, x, core), head: 1.
Axes of the slice: x: 2, y: 2, z: 4, core: 2. Of those that a mesh axis runs over, the one named last changes fastest.
Arguments:
- queries: bfloat16 [4096, 4096], P(('ctx', 'head')), may hold values from -5 to 5
- key_states: bfloat16 [4096, 512], P('ctx', 'head'), may hold values from -5 to 5
- value_states: bfloat16 [4096, 512], P('ctx', 'head'), may hold values from -6 to 6
- outputs: bfloat16 [4096, 4096], P(('ctx', 'head')), may hold values from -6 to 6
- out_grad: bfloat16 [4096, 4096], P(('ctx', 'head')), may hold values from -6 to 6
- doc_of_tile: int32 [32], replicated, may hold values from 0 to 3, never falling along the last dimension, each value on 1 to 16 neighbouring positions
- tile_position: int32 [32], replicated, may hold values from 0 to 31, each once
Outputs:
- query_grad: bfloat16 [4096, 4096], P('ctx', 'head')
- key_grad: bfloat16 [4096, 512], P('ctx', 'head')
- value_grad: bfloat16 [4096, 512], P('ctx', 'head')
The draws below stay inside these ranges and needn't reach their ends.
Inputs may be any that keep to these rules, and one draw needn't show every extreme that they name: `doc_of_tile`: each document is a run of whole tiles in sequence order, 1 to 16 tiles long, one exactly 16. `tile_position`: a permutation of the 32 sequence tiles.
All inputs are finite; a program needn't handle non-finite values.
Results may differ from the reference program's by a relative error of at most 0.005.
Values may be sent and summed in bfloat16 or wider, within the bound.
A program may use at most 64 MiB of HBM per device.

```python
import math
import jax
import jax.numpy as jnp
import numpy as np
from jax import lax

HD = 128
HQ = 32
KVH = 4
TILE = 128
TOKENS = 4096
TILES = 32
GROUP = 8
DOCS = 4
DOC_MOST = 16


def drawn_draws(key):
    base_keys = jnp.clip(jax.random.normal(jax.random.fold_in(key, 11), (TOKENS, KVH, HD), jnp.float32), -5.0, 5.0)
    base_queries = jnp.clip(jax.random.normal(jax.random.fold_in(key, 12), (TOKENS, KVH, GROUP, HD), jnp.float32), -5.0, 5.0)
    new_keys = base_keys
    new_queries = base_queries
    return (new_queries.reshape(TOKENS, HQ * HD), new_keys.reshape(TOKENS, KVH * HD))


def draw_queries(key, part):
    return drawn_draws(key)[0].astype(jnp.bfloat16)


def draw_key_states(key, part):
    return drawn_draws(key)[1].astype(jnp.bfloat16)


def steps_of(own_key, extent, split, least, high):
    def one(position, blocks):
        heights = jax.random.uniform(jax.random.fold_in(jax.random.fold_in(own_key, 6), position), (blocks,), jnp.float32, least / len(split), high / len(split))
        return jnp.repeat(jnp.exp(heights), extent[position] // blocks).reshape((-1,) + (1,) * (len(extent) - position - 1))

    gain = one(*split[0])
    for cut in split[1:]:
        gain = gain * one(*cut)
    return gain


def split_up(number_of, total, limit, lean):
    weights = [(1 << 20) // math.isqrt(standing ** lean) + 1 for standing in range(2, number_of + 1)]
    surplus, given = total - limit - (number_of - 1), [1] * (number_of - 1)
    while surplus > 0:
        candidates = [i for i in range(number_of - 1) if given[i] < limit]
        whole, left = sum([weights[i] for i in candidates]), surplus
        for i in candidates:
            extra = min(limit - given[i], max(1, left * weights[i] // whole), surplus)
            given[i] = given[i] + extra
            surplus = surplus - extra
    return np.array([limit] + given)


def uneven(stream_key, amount, total, bound, skew):
    if amount == 2:
        one = jax.random.randint(stream_key, (), max(1, total - bound), min(bound, total - 1) + 1)
        return jnp.stack([one, total - one])
    sizes = jnp.asarray(split_up(amount, total, bound, skew), jnp.int32)
    twos = (amount - 1) // 2
    giver, sink = sizes[1:1 + 2 * twos:2], sizes[2:2 + 2 * twos:2]
    slack = jnp.minimum(giver - 1, bound - sink)
    shifted = jax.random.randint(jax.random.fold_in(stream_key, 1), (twos,), 0, 1 << 20) % (slack + 1)
    sizes = sizes.at[1:1 + 2 * twos:2].set(giver - shifted).at[2:2 + 2 * twos:2].set(sink + shifted)
    return sizes[jax.random.permutation(jax.random.fold_in(stream_key, 2), amount)]


def gaussian(rng, extent, spread, reach, pieces=(), kind=jnp.bfloat16):
    gain = steps_of(rng, extent, pieces, -0.22, 0.18) if pieces else 1.0
    entries = jax.random.normal(rng, extent, jnp.float32) * spread * gain
    return jnp.minimum(jnp.maximum(entries, -reach), reach).astype(kind)


def setup_inputs(seed: int = 0) -> dict:
    key_of = jax.random.split(jax.random.key(seed), 8)
    return {
        "queries": draw_queries(jax.random.fold_in(key_of[7], 71), 0),
        "key_states": draw_key_states(jax.random.fold_in(key_of[7], 71), 0),
        "value_states": gaussian(key_of[2], (TOKENS, KVH * HD), 1.0, 6.0, ((0, 32),)),
        "outputs": gaussian(key_of[3], (TOKENS, HQ * HD), 1.0, 6.0, ((0, 32),)),
        "out_grad": gaussian(key_of[4], (TOKENS, HQ * HD), 1.0, 6.0, ((0, 32),)),
        "doc_of_tile": jnp.searchsorted(jnp.cumsum(uneven(key_of[5], DOCS, TILES, DOC_MOST, 2)), jnp.arange(TILES), side="right").astype(jnp.int32),
        "tile_position": jax.random.permutation(key_of[6], TILES).astype(jnp.int32),
    }


def token_layout(tile_position, doc_of_tile):
    row_ids = jnp.arange(TOKENS, dtype=jnp.int32)
    placed = tile_position[row_ids // TILE]
    return placed * TILE + row_ids % TILE, doc_of_tile[placed]


def reference(queries, key_states, value_states, outputs, out_grad, doc_of_tile, tile_position):
    score_scale = HD ** -0.5
    highest = lax.Precision.HIGHEST
    positions, documents = token_layout(tile_position, doc_of_tile)
    query_heads = queries.astype(jnp.float32).reshape(TOKENS, KVH, GROUP, HD)
    grad_heads = out_grad.astype(jnp.float32).reshape(TOKENS, KVH, GROUP, HD)
    output_heads = outputs.astype(jnp.float32).reshape(TOKENS, KVH, GROUP, HD)
    key_heads = key_states.astype(jnp.float32).reshape(TOKENS, KVH, HD)
    value_heads = value_states.astype(jnp.float32).reshape(TOKENS, KVH, HD)
    delta_all = jnp.sum(grad_heads * output_heads, axis=-1)

    def tile_step(carry, tile_index):
        key_sum, value_sum = carry
        first = (tile_index * TILE).astype(jnp.int32)
        query_tile = lax.dynamic_slice_in_dim(query_heads, first, TILE, 0)
        grad_tile = lax.dynamic_slice_in_dim(grad_heads, first, TILE, 0)
        delta_tile = jnp.transpose(lax.dynamic_slice_in_dim(delta_all, first, TILE, 0), (1, 2, 0))
        query_pos = lax.dynamic_slice_in_dim(positions, first, TILE, 0)
        query_doc = lax.dynamic_slice_in_dim(documents, first, TILE, 0)
        visible = (query_doc[:, None] == documents[None, :]) & (positions[None, :] <= query_pos[:, None])
        scores = jnp.einsum("qkgd,pkd->kgqp", query_tile, key_heads, precision=highest) * score_scale
        top = jnp.max(jnp.where(visible, scores, -1e30), axis=-1)
        total = jnp.sum(jnp.exp(jnp.where(visible, scores - top[..., None], -1e30)), axis=-1)
        log_total = top + jnp.log(total)
        probs = jnp.exp(jnp.where(visible, scores - log_total[..., None], -1e30))
        probs_low = lax.optimization_barrier(probs.astype(jnp.bfloat16)).astype(jnp.float32)
        grad_probs = jnp.einsum("qkgd,pkd->kgqp", grad_tile, value_heads, precision=highest)
        grad_scores = probs * (grad_probs - delta_tile[..., None]) * score_scale
        grad_scores = lax.optimization_barrier(grad_scores.astype(jnp.bfloat16)).astype(jnp.float32)
        query_part = jnp.einsum("kgqp,pkd->qkgd", grad_scores, key_heads, precision=highest)
        key_sum = key_sum + jnp.einsum("kgqp,qkgd->pkd", grad_scores, query_tile, precision=highest)
        value_sum = value_sum + jnp.einsum("kgqp,qkgd->pkd", probs_low, grad_tile, precision=highest)
        return (key_sum, value_sum), query_part.astype(jnp.bfloat16).reshape(TILE, HQ * HD)

    zeros_start = jnp.zeros((TOKENS, KVH, HD), jnp.float32)
    (key_sum, value_sum), query_parts = lax.scan(tile_step, (zeros_start, zeros_start), jnp.arange(TILES))
    query_grad = query_parts.reshape(TOKENS, HQ * HD)
    key_grad = key_sum.reshape(TOKENS, KVH * HD).astype(jnp.bfloat16)
    value_grad = value_sum.reshape(TOKENS, KVH * HD).astype(jnp.bfloat16)
    return (query_grad, key_grad, value_grad)
```

```python
import functools

import jax
import jax.numpy as jnp
from jax import lax
from jax.experimental import pallas as pl
from jax.experimental.pallas import tpu as pltpu
from jax.sharding import PartitionSpec as P

HD = 128
TILE = 128
SPAN = 2
LOW = -1e30


def kernel(
    heads,
    tiles,
    place_ref,
    place_start_ref,
    inverse_ref,
    qd_ref,
    delta_ref,
    kv_ref,
    dq_ref,
    dkv_ref,
    q_rows,
    q_cols,
    g_rows,
    g_cols,
    score_buf,
    dq_acc,
):
    width = heads * HD
    scale = HD ** (-0.5)
    keys = SPAN * TILE
    dkv_ref[...] = jnp.zeros_like(dkv_ref)
    row_id = lax.broadcasted_iota(jnp.int32, (keys, width), 0)
    col_id = lax.broadcasted_iota(jnp.int32, (keys, width), 1) & (TILE - 1)
    gap = row_id - col_id

    def spots(last):
        found = []
        for offset in range(SPAN):
            where = jnp.maximum(last - (SPAN - 1) + offset, 0)
            found.append(pl.multiple_of(inverse_ref[where] * TILE, TILE))
        return found

    def block(last, begin):
        return jnp.concatenate(
            [kv_ref[pl.ds(spot, TILE), begin : begin + HD] for spot in spots(last)], axis=0
        )

    @pl.loop(0, tiles)
    def _(tile):
        first_row = pl.multiple_of(tile * TILE, TILE)
        place = place_ref[tile]
        start = place_start_ref[tile]
        chunks = (place - start + SPAN) // SPAN
        for h in range(heads):
            lanes = slice(h * HD, (h + 1) * HD)
            q_block = qd_ref[pl.ds(first_row, TILE), h * HD : (h + 1) * HD]
            g_block = qd_ref[pl.ds(first_row, TILE), width + h * HD : width + (h + 1) * HD]
            q_rows[lanes, :] = q_block
            g_rows[lanes, :] = g_block
            q_cols[:, lanes] = q_block.T
            g_cols[:, lanes] = g_block.T

        def totals(step, state):
            top, total = state
            last = place - SPAN * step
            scores = (
                jnp.dot(block(last, 0), q_cols[...], preferred_element_type=jnp.float32) * scale
            )
            first_key = (last - (SPAN - 1)) * TILE
            visible = (gap <= place * TILE - first_key) & (row_id >= start * TILE - first_key)
            scores = jnp.where(visible, scores, LOW)
            score_buf[step] = scores
            new_top = jnp.maximum(top, jnp.max(scores, axis=0, keepdims=True))
            total = total * jnp.exp(top - new_top) + jnp.sum(
                jnp.exp(scores - new_top), axis=0, keepdims=True
            )
            return new_top, total

        top, total = lax.fori_loop(
            0,
            chunks,
            totals,
            (jnp.full((1, width), LOW, jnp.float32), jnp.zeros((1, width), jnp.float32)),
        )
        log_total = top + jnp.log(total)
        delta = delta_ref[tile]
        dq_acc[...] = jnp.zeros_like(dq_acc)

        @pl.loop(0, chunks)
        def _(step):
            last = place - SPAN * step
            k_block = block(last, 0)
            probs = jnp.exp(score_buf[step] - log_total)
            grad_probs = jnp.dot(
                block(last, HD), g_cols[...], preferred_element_type=jnp.float32
            )
            low = probs.astype(jnp.bfloat16)
            grad_scores = (probs * (grad_probs - delta) * scale).astype(jnp.bfloat16)
            dv = jnp.dot(low, g_rows[...], preferred_element_type=jnp.float32)
            dk = jnp.dot(grad_scores, q_rows[...], preferred_element_type=jnp.float32)
            dq_acc[...] += lax.dot_general(
                k_block,
                grad_scores,
                (((0,), (0,)), ((), ())),
                preferred_element_type=jnp.float32,
            )
            for offset, spot in enumerate(spots(last)):
                rows = slice(offset * TILE, (offset + 1) * TILE)
                dkv_ref[pl.ds(spot, TILE), 0:HD] += dk[rows]
                dkv_ref[pl.ds(spot, TILE), HD : 2 * HD] += dv[rows]

        for h in range(heads):
            lanes = slice(h * HD, (h + 1) * HD)
            dq_ref[pl.ds(first_row, TILE), lanes] = dq_acc[:, lanes].T.astype(jnp.bfloat16)


def attention_backward(places, starts, inverse, qd, delta, kv):
    rows, both = qd.shape
    width = both // 2
    heads = width // HD
    tokens = kv.shape[0]
    tiles = rows // TILE
    steps = tokens // TILE // SPAN
    smem = pl.BlockSpec(memory_space=pltpu.SMEM)
    vmem = pl.BlockSpec(memory_space=pltpu.VMEM)
    return pl.pallas_call(
        functools.partial(kernel, heads, tiles),
        out_shape=(
            jax.ShapeDtypeStruct((rows, width), jnp.bfloat16),
            jax.ShapeDtypeStruct((tokens, 2 * HD), jnp.float32),
        ),
        in_specs=[smem, smem, smem, vmem, vmem, vmem],
        out_specs=(vmem, vmem),
        scratch_shapes=[
            pltpu.VMEM((width, HD), jnp.bfloat16),
            pltpu.VMEM((HD, width), jnp.bfloat16),
            pltpu.VMEM((width, HD), jnp.bfloat16),
            pltpu.VMEM((HD, width), jnp.bfloat16),
            pltpu.VMEM((steps // 2 + 1, SPAN * TILE, width), jnp.float32),
            pltpu.VMEM((HD, width), jnp.float32),
        ],
        compiler_params=pltpu.CompilerParams(vmem_limit_bytes=48 * 1024 * 1024),
        cost_estimate=pl.CostEstimate(
            flops=rows * width * tokens * 3, bytes_accessed=12 << 20, transcendentals=0
        ),
    )(places, starts, inverse, qd, delta, kv)


def local(queries, key_states, value_states, outputs, out_grad, doc_of_tile, tile_position):
    rows = queries.shape[0]
    kv_heads = key_states.shape[1] // HD
    head_count = lax.axis_size("head")
    ctx_count = lax.axis_size("ctx")
    ctx_index = lax.axis_index("ctx")
    split = kv_heads * head_count
    team = kv_heads
    near = [[b * team + s for s in range(team)] for b in range(ctx_count // team)]
    far = [[b * team + s for b in range(ctx_count // team)] for s in range(team)]

    def swap(value, split_axis, concat_axis):
        if head_count > 1:
            return lax.all_to_all(value, "head", split_axis, concat_axis, tiled=True)
        return lax.all_to_all(
            value, "ctx", split_axis, concat_axis, axis_index_groups=near, tiled=True
        )

    heads = queries.shape[1] // split // HD
    products = out_grad.astype(jnp.float32) * outputs.astype(jnp.float32)
    delta = jnp.sum(products.reshape(rows, split * heads, HD), axis=-1)
    if head_count == 1:
        kv = jnp.concatenate(
            [key_states.reshape(rows, split, HD), value_states.reshape(rows, split, HD)], axis=2
        ).reshape(rows, split * 2 * HD)
        kv = swap(kv, 1, 0)
    else:
        kv = jnp.concatenate([key_states, value_states], axis=1)
    kv_all = lax.all_gather(kv, "ctx", axis=0, tiled=True, axis_index_groups=far)
    qd = jnp.concatenate(
        [
            queries.reshape(rows, split, heads * HD),
            out_grad.reshape(rows, split, heads * HD),
        ],
        axis=2,
    ).reshape(rows, split * 2 * heads * HD)
    qd = swap(qd, 1, 0)
    delta = swap(delta, 1, 0)
    many = qd.shape[0]
    tiles = many // TILE
    delta = jnp.transpose(delta.reshape(tiles, TILE, heads), (0, 2, 1)).reshape(
        tiles, 1, heads * TILE
    )
    count = tile_position.shape[0]
    order = jnp.arange(count, dtype=jnp.int32)
    inverse = jnp.sum(
        jnp.where(tile_position[None, :] == order[:, None], order[None, :], 0), axis=1
    ).astype(jnp.int32)
    places = lax.dynamic_slice_in_dim(tile_position, (ctx_index // team) * tiles, tiles)
    starts = jnp.sum(
        (doc_of_tile[None, :] < doc_of_tile[places][:, None]).astype(jnp.int32), axis=1
    ).astype(jnp.int32)
    dq, dkv = attention_backward(places, starts, inverse, qd, delta, kv_all)
    dkv = lax.psum_scatter(
        dkv, "ctx", scatter_dimension=0, axis_index_groups=far, tiled=True
    ).astype(jnp.bfloat16)
    if head_count == 1:
        dq = swap(dq, 0, 1)
        dkv = swap(dkv, 0, 1)
    dkv = dkv.reshape(dkv.shape[0], kv_heads, 2, HD)
    width = kv_heads * HD
    return (
        dq,
        dkv[:, :, 0].reshape(-1, width),
        dkv[:, :, 1].reshape(-1, width),
    )


def solution(mesh):
    placed = (
        P(("ctx", "head"), None),
        P("ctx", "head"),
        P("ctx", "head"),
        P(("ctx", "head"), None),
        P(("ctx", "head"), None),
        P(),
        P(),
    )
    return jax.shard_map(
        local,
        mesh=mesh,
        in_specs=placed,
        out_specs=(P("ctx", "head"), P("ctx", "head"), P("ctx", "head")),
        check_vma=False,
    )
```

```python
import functools

import jax
import jax.numpy as jnp
from jax import lax
from jax.experimental import pallas as pl
from jax.experimental.pallas import tpu as pltpu
from jax.sharding import PartitionSpec as P

HD = 128
TILE = 128
SPAN = 2
LOW = -1e30


def kernel(
    heads,
    tiles,
    place_ref,
    place_start_ref,
    inverse_ref,
    qd_ref,
    delta_ref,
    kv_ref,
    dq_ref,
    dkv_ref,
    q_rows,
    q_cols,
    g_rows,
    g_cols,
    score_buf,
    dq_acc,
    dkv_acc,
):
    width = heads * HD
    scale = HD ** (-0.5)
    keys = SPAN * TILE
    dkv_acc[...] = jnp.zeros_like(dkv_acc)
    row_id = lax.broadcasted_iota(jnp.int32, (keys, width), 0)
    col_id = lax.broadcasted_iota(jnp.int32, (keys, width), 1) & (TILE - 1)
    gap = row_id - col_id

    def spots(last):
        found = []
        for offset in range(SPAN):
            where = jnp.maximum(last - (SPAN - 1) + offset, 0)
            found.append(pl.multiple_of(inverse_ref[where] * TILE, TILE))
        return found

    def block(last, begin):
        return jnp.concatenate(
            [kv_ref[pl.ds(spot, TILE), begin : begin + HD] for spot in spots(last)], axis=0
        )

    @pl.loop(0, tiles)
    def _(tile):
        first_row = pl.multiple_of(tile * TILE, TILE)
        place = place_ref[tile]
        start = place_start_ref[tile]
        chunks = (place - start + SPAN) // SPAN
        for h in range(heads):
            lanes = slice(h * HD, (h + 1) * HD)
            q_block = qd_ref[pl.ds(first_row, TILE), h * HD : (h + 1) * HD]
            g_block = qd_ref[pl.ds(first_row, TILE), width + h * HD : width + (h + 1) * HD]
            q_rows[lanes, :] = q_block
            g_rows[lanes, :] = g_block
            q_cols[:, lanes] = q_block.T
            g_cols[:, lanes] = g_block.T

        def totals(step, state):
            top, total = state
            last = place - SPAN * step
            scores = (
                jnp.dot(block(last, 0), q_cols[...], preferred_element_type=jnp.float32) * scale
            )
            first_key = (last - (SPAN - 1)) * TILE
            visible = (gap <= place * TILE - first_key) & (row_id >= start * TILE - first_key)
            scores = jnp.where(visible, scores, LOW)
            score_buf[step] = scores
            new_top = jnp.maximum(top, jnp.max(scores, axis=0, keepdims=True))
            total = total * jnp.exp(top - new_top) + jnp.sum(
                jnp.exp(scores - new_top), axis=0, keepdims=True
            )
            return new_top, total

        top, total = lax.fori_loop(
            0,
            chunks,
            totals,
            (jnp.full((1, width), LOW, jnp.float32), jnp.zeros((1, width), jnp.float32)),
        )
        log_total = top + jnp.log(total)
        delta = delta_ref[tile]
        dq_acc[...] = jnp.zeros_like(dq_acc)

        @pl.loop(0, chunks)
        def _(step):
            last = place - SPAN * step
            k_block = block(last, 0)
            probs = jnp.exp(score_buf[step] - log_total)
            grad_probs = jnp.dot(
                block(last, HD), g_cols[...], preferred_element_type=jnp.float32
            )
            low = probs.astype(jnp.bfloat16)
            grad_scores = (probs * (grad_probs - delta) * scale).astype(jnp.bfloat16)
            dv = jnp.dot(low, g_rows[...], preferred_element_type=jnp.float32)
            dk = jnp.dot(grad_scores, q_rows[...], preferred_element_type=jnp.float32)
            dq_acc[...] += lax.dot_general(
                k_block,
                grad_scores,
                (((0,), (0,)), ((), ())),
                preferred_element_type=jnp.float32,
            )
            for offset, spot in enumerate(spots(last)):
                rows = slice(offset * TILE, (offset + 1) * TILE)
                dkv_acc[pl.ds(spot, TILE), 0:HD] += dk[rows]
                dkv_acc[pl.ds(spot, TILE), HD : 2 * HD] += dv[rows]

        for h in range(heads):
            lanes = slice(h * HD, (h + 1) * HD)
            dq_ref[pl.ds(first_row, TILE), lanes] = dq_acc[:, lanes].T.astype(jnp.bfloat16)

    dkv_ref[...] = dkv_acc[...].astype(jnp.bfloat16)


def attention_backward(places, starts, inverse, qd, delta, kv):
    rows, both = qd.shape
    width = both // 2
    heads = width // HD
    tokens = kv.shape[0]
    tiles = rows // TILE
    steps = tokens // TILE // SPAN
    smem = pl.BlockSpec(memory_space=pltpu.SMEM)
    vmem = pl.BlockSpec(memory_space=pltpu.VMEM)
    return pl.pallas_call(
        functools.partial(kernel, heads, tiles),
        out_shape=(
            jax.ShapeDtypeStruct((rows, width), jnp.bfloat16),
            jax.ShapeDtypeStruct((tokens, 2 * HD), jnp.bfloat16),
        ),
        in_specs=[smem, smem, smem, vmem, vmem, vmem],
        out_specs=(vmem, vmem),
        scratch_shapes=[
            pltpu.VMEM((width, HD), jnp.bfloat16),
            pltpu.VMEM((HD, width), jnp.bfloat16),
            pltpu.VMEM((width, HD), jnp.bfloat16),
            pltpu.VMEM((HD, width), jnp.bfloat16),
            pltpu.VMEM((steps // 2 + 1, SPAN * TILE, width), jnp.float32),
            pltpu.VMEM((HD, width), jnp.float32),
            pltpu.VMEM((tokens, 2 * HD), jnp.float32),
        ],
        compiler_params=pltpu.CompilerParams(vmem_limit_bytes=48 * 1024 * 1024),
        cost_estimate=pl.CostEstimate(
            flops=rows * width * tokens * 3, bytes_accessed=12 << 20, transcendentals=0
        ),
    )(places, starts, inverse, qd, delta, kv)


def local(queries, key_states, value_states, outputs, out_grad, doc_of_tile, tile_position):
    rows = queries.shape[0]
    kv_heads = key_states.shape[1] // HD
    head_count = lax.axis_size("head")
    ctx_count = lax.axis_size("ctx")
    ctx_index = lax.axis_index("ctx")
    split = kv_heads * head_count
    team = kv_heads
    near = [[b * team + s for s in range(team)] for b in range(ctx_count // team)]
    far = [[b * team + s for b in range(ctx_count // team)] for s in range(team)]

    def swap(value, split_axis, concat_axis):
        if head_count > 1:
            return lax.all_to_all(value, "head", split_axis, concat_axis, tiled=True)
        return lax.all_to_all(
            value, "ctx", split_axis, concat_axis, axis_index_groups=near, tiled=True
        )

    heads = queries.shape[1] // split // HD
    products = out_grad.astype(jnp.float32) * outputs.astype(jnp.float32)
    delta = jnp.sum(products.reshape(rows, split * heads, HD), axis=-1)
    if head_count == 1:
        kv = jnp.concatenate(
            [key_states.reshape(rows, split, HD), value_states.reshape(rows, split, HD)], axis=2
        ).reshape(rows, split * 2 * HD)
        kv = swap(kv, 1, 0)
    else:
        kv = jnp.concatenate([key_states, value_states], axis=1)
    kv_all = lax.all_gather(kv, "ctx", axis=0, tiled=True, axis_index_groups=far)
    qd = jnp.concatenate(
        [
            queries.reshape(rows, split, heads * HD),
            out_grad.reshape(rows, split, heads * HD),
        ],
        axis=2,
    ).reshape(rows, split * 2 * heads * HD)
    qd = swap(qd, 1, 0)
    delta = swap(delta, 1, 0)
    many = qd.shape[0]
    tiles = many // TILE
    delta = jnp.transpose(delta.reshape(tiles, TILE, heads), (0, 2, 1)).reshape(
        tiles, 1, heads * TILE
    )
    count = tile_position.shape[0]
    order = jnp.arange(count, dtype=jnp.int32)
    inverse = jnp.sum(
        jnp.where(tile_position[None, :] == order[:, None], order[None, :], 0), axis=1
    ).astype(jnp.int32)
    places = lax.dynamic_slice_in_dim(tile_position, (ctx_index // team) * tiles, tiles)
    starts = jnp.sum(
        (doc_of_tile[None, :] < doc_of_tile[places][:, None]).astype(jnp.int32), axis=1
    ).astype(jnp.int32)
    dq, dkv = attention_backward(places, starts, inverse, qd, delta, kv_all)
    parts = ctx_count // team
    dkv = lax.all_to_all(dkv, "ctx", 0, 0, axis_index_groups=far, tiled=True)
    dkv = jnp.sum(dkv.reshape(parts, -1, 2 * HD).astype(jnp.float32), axis=0).astype(jnp.bfloat16)
    if head_count == 1:
        dq = swap(dq, 0, 1)
        dkv = swap(dkv, 0, 1)
    dkv = dkv.reshape(dkv.shape[0], kv_heads, 2, HD)
    width = kv_heads * HD
    return (
        dq,
        dkv[:, :, 0].reshape(-1, width),
        dkv[:, :, 1].reshape(-1, width),
    )


def solution(mesh):
    placed = (
        P(("ctx", "head"), None),
        P("ctx", "head"),
        P("ctx", "head"),
        P(("ctx", "head"), None),
        P(("ctx", "head"), None),
        P(),
        P(),
    )
    return jax.shard_map(
        local,
        mesh=mesh,
        in_specs=placed,
        out_specs=(P("ctx", "head"), P("ctx", "head"), P("ctx", "head")),
        check_vma=False,
    )
```

```python
import functools

import jax
import jax.numpy as jnp
from jax import lax
from jax.experimental import pallas as pl
from jax.experimental.pallas import tpu as pltpu
from jax.sharding import PartitionSpec as P

HD = 128
TILE = 128
SPAN = 2
LOW = -1e30


def kernel(
    heads,
    tiles,
    place_ref,
    place_start_ref,
    inverse_ref,
    qd_ref,
    delta_ref,
    kv_ref,
    dq_ref,
    dkv_ref,
    q_rows,
    q_cols,
    g_rows,
    g_cols,
    score_buf,
    dq_acc,
    dkv_acc,
):
    width = heads * HD
    scale = HD ** (-0.5)
    keys = SPAN * TILE
    dkv_acc[...] = jnp.zeros_like(dkv_acc)
    row_id = lax.broadcasted_iota(jnp.int32, (keys, width), 0)
    col_id = lax.broadcasted_iota(jnp.int32, (keys, width), 1) & (TILE - 1)
    gap = row_id - col_id

    def spots(last):
        found = []
        for offset in range(SPAN):
            where = jnp.maximum(last - (SPAN - 1) + offset, 0)
            found.append(pl.multiple_of(inverse_ref[where] * TILE, TILE))
        return found

    def block(last, begin):
        return jnp.concatenate(
            [kv_ref[pl.ds(spot, TILE), begin : begin + HD] for spot in spots(last)], axis=0
        )

    @pl.loop(0, tiles)
    def _(tile):
        first_row = pl.multiple_of(tile * TILE, TILE)
        place = place_ref[tile]
        start = place_start_ref[tile]
        chunks = (place - start + SPAN) // SPAN
        for h in range(heads):
            lanes = slice(h * HD, (h + 1) * HD)
            q_block = qd_ref[pl.ds(first_row, TILE), h * HD : (h + 1) * HD]
            g_block = qd_ref[pl.ds(first_row, TILE), width + h * HD : width + (h + 1) * HD]
            q_rows[lanes, :] = q_block
            g_rows[lanes, :] = g_block
            q_cols[:, lanes] = q_block.T
            g_cols[:, lanes] = g_block.T

        def totals(step, state):
            top, total = state
            last = place - SPAN * step
            scores = (
                jnp.dot(block(last, 0), q_cols[...], preferred_element_type=jnp.float32) * scale
            )
            first_key = (last - (SPAN - 1)) * TILE
            visible = (gap <= place * TILE - first_key) & (row_id >= start * TILE - first_key)
            scores = jnp.where(visible, scores, LOW)
            score_buf[step] = scores
            new_top = jnp.maximum(top, jnp.max(scores, axis=0, keepdims=True))
            total = total * jnp.exp(top - new_top) + jnp.sum(
                jnp.exp(scores - new_top), axis=0, keepdims=True
            )
            return new_top, total

        top, total = lax.fori_loop(
            0,
            chunks,
            totals,
            (jnp.full((1, width), LOW, jnp.float32), jnp.zeros((1, width), jnp.float32)),
        )
        log_total = top + jnp.log(total)
        delta = delta_ref[tile]
        dq_acc[...] = jnp.zeros_like(dq_acc)

        @pl.loop(0, chunks)
        def _(step):
            last = place - SPAN * step
            k_block = block(last, 0)
            probs = jnp.exp(score_buf[step] - log_total)
            grad_probs = jnp.dot(
                block(last, HD), g_cols[...], preferred_element_type=jnp.float32
            )
            low = probs.astype(jnp.bfloat16)
            grad_scores = (probs * (grad_probs - delta) * scale).astype(jnp.bfloat16)
            dv = jnp.dot(low, g_rows[...], preferred_element_type=jnp.float32)
            dk = jnp.dot(grad_scores, q_rows[...], preferred_element_type=jnp.float32)
            dq_acc[...] += lax.dot_general(
                k_block,
                grad_scores,
                (((0,), (0,)), ((), ())),
                preferred_element_type=jnp.float32,
            )
            for offset, spot in enumerate(spots(last)):
                rows = slice(offset * TILE, (offset + 1) * TILE)
                dkv_acc[pl.ds(spot, TILE), 0:HD] += dk[rows]
                dkv_acc[pl.ds(spot, TILE), HD : 2 * HD] += dv[rows]

        for h in range(heads):
            lanes = slice(h * HD, (h + 1) * HD)
            dq_ref[pl.ds(first_row, TILE), lanes] = dq_acc[:, lanes].T.astype(jnp.bfloat16)

    dkv_ref[...] = dkv_acc[...].astype(jnp.bfloat16)


def attention_backward(places, starts, inverse, qd, delta, kv):
    rows, both = qd.shape
    width = both // 2
    heads = width // HD
    tokens = kv.shape[0]
    tiles = rows // TILE
    steps = tokens // TILE // SPAN
    smem = pl.BlockSpec(memory_space=pltpu.SMEM)
    vmem = pl.BlockSpec(memory_space=pltpu.VMEM)
    return pl.pallas_call(
        functools.partial(kernel, heads, tiles),
        out_shape=(
            jax.ShapeDtypeStruct((rows, width), jnp.bfloat16),
            jax.ShapeDtypeStruct((tokens, 2 * HD), jnp.bfloat16),
        ),
        in_specs=[smem, smem, smem, vmem, vmem, vmem],
        out_specs=(vmem, vmem),
        scratch_shapes=[
            pltpu.VMEM((width, HD), jnp.bfloat16),
            pltpu.VMEM((HD, width), jnp.bfloat16),
            pltpu.VMEM((width, HD), jnp.bfloat16),
            pltpu.VMEM((HD, width), jnp.bfloat16),
            pltpu.VMEM((steps // 2 + 1, SPAN * TILE, width), jnp.float32),
            pltpu.VMEM((HD, width), jnp.float32),
            pltpu.VMEM((tokens, 2 * HD), jnp.float32),
        ],
        compiler_params=pltpu.CompilerParams(vmem_limit_bytes=48 * 1024 * 1024),
        cost_estimate=pl.CostEstimate(
            flops=rows * width * tokens * 3, bytes_accessed=12 << 20, transcendentals=0
        ),
    )(places, starts, inverse, qd, delta, kv)


def local(queries, key_states, value_states, outputs, out_grad, doc_of_tile, tile_position):
    rows = queries.shape[0]
    kv_heads = key_states.shape[1] // HD
    head_count = lax.axis_size("head")
    ctx_count = lax.axis_size("ctx")
    ctx_index = lax.axis_index("ctx")
    split = kv_heads * head_count
    team = kv_heads
    near = [[b * team + s for s in range(team)] for b in range(ctx_count // team)]
    far = [[b * team + s for b in range(ctx_count // team)] for s in range(team)]

    def swap(value, split_axis, concat_axis):
        if head_count > 1:
            return lax.all_to_all(value, "head", split_axis, concat_axis, tiled=True)
        return lax.all_to_all(
            value, "ctx", split_axis, concat_axis, axis_index_groups=near, tiled=True
        )

    heads = queries.shape[1] // split // HD
    products = out_grad.astype(jnp.float32) * outputs.astype(jnp.float32)
    delta = jnp.sum(products.reshape(rows, split * heads, HD), axis=-1)
    if head_count == 1:
        kv = jnp.concatenate(
            [key_states.reshape(rows, split, HD), value_states.reshape(rows, split, HD)], axis=2
        ).reshape(rows, split * 2 * HD)
        kv = swap(kv, 1, 0)
    else:
        kv = jnp.concatenate([key_states, value_states], axis=1)
    kv_all = lax.all_gather(kv, "ctx", axis=0, tiled=True, axis_index_groups=far)
    qd = jnp.concatenate(
        [
            queries.reshape(rows, split, heads * HD),
            out_grad.reshape(rows, split, heads * HD),
        ],
        axis=2,
    ).reshape(rows, split * 2 * heads * HD)
    qd = swap(qd, 1, 0)
    delta = swap(delta, 1, 0)
    many = qd.shape[0]
    tiles = many // TILE
    delta = jnp.transpose(delta.reshape(tiles, TILE, heads), (0, 2, 1)).reshape(
        tiles, 1, heads * TILE
    )
    count = tile_position.shape[0]
    order = jnp.arange(count, dtype=jnp.int32)
    inverse = jnp.sum(
        jnp.where(tile_position[None, :] == order[:, None], order[None, :], 0), axis=1
    ).astype(jnp.int32)
    places = lax.dynamic_slice_in_dim(tile_position, (ctx_index // team) * tiles, tiles)
    starts = jnp.sum(
        (doc_of_tile[None, :] < doc_of_tile[places][:, None]).astype(jnp.int32), axis=1
    ).astype(jnp.int32)
    dq, dkv = attention_backward(places, starts, inverse, qd, delta, kv_all)
    parts = ctx_count // team
    if head_count == 1:
        blocks = dq.reshape(team, rows, -1)
        me = ctx_index & (team - 1)
        home = jnp.zeros_like(blocks)
        for shift in range(team):
            piece = lax.dynamic_index_in_dim(blocks, me ^ shift, 0)
            if shift:
                pairs = [(i, i ^ shift) for i in range(ctx_count)]
                piece = lax.ppermute(piece, "ctx", pairs)
            home = lax.dynamic_update_slice_in_dim(home, piece, me ^ shift, 0)
        dq_home = jnp.transpose(home, (1, 0, 2)).reshape(rows, -1)
    dkv = lax.all_to_all(dkv, "ctx", 0, 0, axis_index_groups=far, tiled=True)
    dkv = jnp.sum(dkv.reshape(parts, -1, 2 * HD).astype(jnp.float32), axis=0).astype(jnp.bfloat16)
    if head_count == 1:
        dkv = swap(dkv, 0, 1)
        dq = dq_home
    dkv = dkv.reshape(dkv.shape[0], kv_heads, 2, HD)
    width = kv_heads * HD
    return (
        dq,
        dkv[:, :, 0].reshape(-1, width),
        dkv[:, :, 1].reshape(-1, width),
    )


def solution(mesh):
    placed = (
        P(("ctx", "head"), None),
        P("ctx", "head"),
        P("ctx", "head"),
        P(("ctx", "head"), None),
        P(("ctx", "head"), None),
        P(),
        P(),
    )
    return jax.shard_map(
        local,
        mesh=mesh,
        in_specs=placed,
        out_specs=(P("ctx", "head"), P("ctx", "head"), P("ctx", "head")),
        check_vma=False,
    )
```

```python
import functools

import jax
import jax.numpy as jnp
from jax import lax
from jax.experimental import pallas as pl
from jax.experimental.pallas import tpu as pltpu
from jax.sharding import PartitionSpec as P

HD = 128
TILE = 128
SPAN = 2
LOW = -1e30


def kernel(
    heads,
    tiles,
    place_ref,
    place_start_ref,
    inverse_ref,
    qd_ref,
    delta_ref,
    kv_ref,
    dq_ref,
    dkv_ref,
    q_rows,
    q_cols,
    g_rows,
    g_cols,
    score_buf,
    dq_acc,
    dkv_acc,
):
    width = heads * HD
    scale = HD ** (-0.5)
    keys = SPAN * TILE
    dkv_acc[...] = jnp.zeros_like(dkv_acc)
    row_id = lax.broadcasted_iota(jnp.int32, (keys, width), 0)
    col_id = lax.broadcasted_iota(jnp.int32, (keys, width), 1) & (TILE - 1)
    gap = row_id - col_id

    def spots(last):
        found = []
        for offset in range(SPAN):
            where = jnp.maximum(last - (SPAN - 1) + offset, 0)
            found.append(pl.multiple_of(inverse_ref[where] * TILE, TILE))
        return found

    def block(last, begin):
        return jnp.concatenate(
            [kv_ref[pl.ds(spot, TILE), begin : begin + HD] for spot in spots(last)], axis=0
        )

    @pl.loop(0, tiles)
    def _(tile):
        first_row = pl.multiple_of(tile * TILE, TILE)
        place = place_ref[tile]
        start = place_start_ref[tile]
        chunks = (place - start + SPAN) // SPAN
        for h in range(heads):
            lanes = slice(h * HD, (h + 1) * HD)
            q_block = qd_ref[pl.ds(first_row, TILE), h * HD : (h + 1) * HD]
            g_block = qd_ref[pl.ds(first_row, TILE), width + h * HD : width + (h + 1) * HD]
            q_rows[lanes, :] = q_block
            g_rows[lanes, :] = g_block
            q_cols[:, lanes] = q_block.T
            g_cols[:, lanes] = g_block.T

        def totals(step, state):
            top, total = state
            last = place - SPAN * step
            scores = (
                jnp.dot(block(last, 0), q_cols[...], preferred_element_type=jnp.float32) * scale
            )
            first_key = (last - (SPAN - 1)) * TILE
            visible = (gap <= place * TILE - first_key) & (row_id >= start * TILE - first_key)
            scores = jnp.where(visible, scores, LOW)
            score_buf[step] = scores
            new_top = jnp.maximum(top, jnp.max(scores, axis=0, keepdims=True))
            total = total * jnp.exp(top - new_top) + jnp.sum(
                jnp.exp(scores - new_top), axis=0, keepdims=True
            )
            return new_top, total

        top, total = lax.fori_loop(
            0,
            chunks,
            totals,
            (jnp.full((1, width), LOW, jnp.float32), jnp.zeros((1, width), jnp.float32)),
        )
        log_total = top + jnp.log(total)
        delta = delta_ref[tile]
        dq_acc[...] = jnp.zeros_like(dq_acc)

        @pl.loop(0, chunks)
        def _(step):
            last = place - SPAN * step
            k_block = block(last, 0)
            probs = jnp.exp(score_buf[step] - log_total)
            grad_probs = jnp.dot(
                block(last, HD), g_cols[...], preferred_element_type=jnp.float32
            )
            low = probs.astype(jnp.bfloat16)
            grad_scores = (probs * (grad_probs - delta) * scale).astype(jnp.bfloat16)
            dv = jnp.dot(low, g_rows[...], preferred_element_type=jnp.float32)
            dk = jnp.dot(grad_scores, q_rows[...], preferred_element_type=jnp.float32)
            dq_acc[...] += lax.dot_general(
                k_block,
                grad_scores,
                (((0,), (0,)), ((), ())),
                preferred_element_type=jnp.float32,
            )
            for offset, spot in enumerate(spots(last)):
                rows = slice(offset * TILE, (offset + 1) * TILE)
                dkv_acc[pl.ds(spot, TILE), 0:HD] += dk[rows]
                dkv_acc[pl.ds(spot, TILE), HD : 2 * HD] += dv[rows]

        for h in range(heads):
            lanes = slice(h * HD, (h + 1) * HD)
            dq_ref[pl.ds(first_row, TILE), lanes] = dq_acc[:, lanes].T.astype(jnp.bfloat16)

    dkv_ref[...] = dkv_acc[...].astype(jnp.bfloat16)


def attention_backward(places, starts, inverse, qd, delta, kv):
    rows, both = qd.shape
    width = both // 2
    heads = width // HD
    tokens = kv.shape[0]
    tiles = rows // TILE
    steps = tokens // TILE // SPAN
    smem = pl.BlockSpec(memory_space=pltpu.SMEM)
    vmem = pl.BlockSpec(memory_space=pltpu.VMEM)
    return pl.pallas_call(
        functools.partial(kernel, heads, tiles),
        out_shape=(
            jax.ShapeDtypeStruct((rows, width), jnp.bfloat16),
            jax.ShapeDtypeStruct((tokens, 2 * HD), jnp.bfloat16),
        ),
        in_specs=[smem, smem, smem, vmem, vmem, vmem],
        out_specs=(vmem, vmem),
        scratch_shapes=[
            pltpu.VMEM((width, HD), jnp.bfloat16),
            pltpu.VMEM((HD, width), jnp.bfloat16),
            pltpu.VMEM((width, HD), jnp.bfloat16),
            pltpu.VMEM((HD, width), jnp.bfloat16),
            pltpu.VMEM((steps // 2 + 1, SPAN * TILE, width), jnp.float32),
            pltpu.VMEM((HD, width), jnp.float32),
            pltpu.VMEM((tokens, 2 * HD), jnp.float32),
        ],
        compiler_params=pltpu.CompilerParams(vmem_limit_bytes=48 * 1024 * 1024),
        cost_estimate=pl.CostEstimate(
            flops=rows * width * tokens * 3, bytes_accessed=12 << 20, transcendentals=0
        ),
    )(places, starts, inverse, qd, delta, kv)


def gather_kernel(parts, team, k_ref, v_ref, out_ref, near_send, near_recv, far_send, far_recv):
    me = lax.axis_index("ctx")
    other = lax.axis_index("head")
    mine = me % team
    block = me // team
    half = parts // 2
    side = block % 2
    turn = (1 - side) * (block // 2) + side * (parts - 1 - block // 2)
    rows = k_ref.shape[0]

    def block_of(place):
        place = (place + parts) % parts
        upper = place // half
        return (1 - upper) * 2 * place + upper * (2 * (parts - 1 - place) + 1)

    right = block_of(turn + 1) * team + mine
    left = block_of(turn - 1) * team + mine
    friends = [block * team + (mine + shift) % team for shift in range(1, team)]
    barrier = pltpu.get_barrier_semaphore()
    for device in [left, right] + friends:
        pl.semaphore_signal(
            barrier, inc=1, device_id=(device, other), device_id_type=pl.DeviceIdType.MESH
        )
    pl.semaphore_wait(barrier, team + 1)
    home = pl.ds(pl.multiple_of(me * rows, TILE), rows)
    copies = []
    for which, ref in enumerate((k_ref, v_ref)):
        lanes = slice(which * HD, (which + 1) * HD)
        for shift in range(1, team):
            source = pl.ds(pl.multiple_of((mine + shift) % team * HD, HD), HD)
            copy = pltpu.make_async_remote_copy(
                src_ref=ref.at[:, source],
                dst_ref=out_ref.at[home, lanes],
                send_sem=near_send.at[which, shift - 1],
                recv_sem=near_recv.at[which, shift - 1],
                device_id=(friends[shift - 1], other),
                device_id_type=pl.DeviceIdType.MESH,
            )
            copy.start()
            copies.append(copy)
    for which, ref in enumerate((k_ref, v_ref)):
        own = pl.ds(pl.multiple_of(mine * HD, HD), HD)
        out_ref[home, which * HD : (which + 1) * HD] = ref[:, own]
    for copy in copies:
        copy.wait_recv()
    span = team * rows
    for step in range(half):
        moves = [(turn - step, right, 0)]
        if step < half - 1:
            moves.append((turn + step, left, 1))
        now = []
        for place, device, way in moves:
            area = pl.ds(pl.multiple_of(block_of(place) * span, TILE), span)
            copy = pltpu.make_async_remote_copy(
                src_ref=out_ref.at[area],
                dst_ref=out_ref.at[area],
                send_sem=far_send.at[way, step],
                recv_sem=far_recv.at[way, step],
                device_id=(device, other),
                device_id_type=pl.DeviceIdType.MESH,
            )
            copy.start()
            now.append(copy)
            copies.append(copy)
        for copy in now:
            copy.wait_recv()
    for copy in copies:
        copy.wait_send()


def gather_head(key_states, value_states, parts, team):
    rows = key_states.shape[0]
    vmem = pl.BlockSpec(memory_space=pltpu.VMEM)
    return pl.pallas_call(
        functools.partial(gather_kernel, parts, team),
        out_shape=jax.ShapeDtypeStruct((parts * team * rows, 2 * HD), jnp.bfloat16),
        in_specs=[vmem, vmem],
        out_specs=vmem,
        scratch_shapes=[
            pltpu.SemaphoreType.DMA((2, team - 1)),
            pltpu.SemaphoreType.DMA((2, team - 1)),
            pltpu.SemaphoreType.DMA((2, parts // 2)),
            pltpu.SemaphoreType.DMA((2, parts // 2)),
        ],
        compiler_params=pltpu.CompilerParams(
            collective_id=0, has_side_effects=True, vmem_limit_bytes=16 * 1024 * 1024
        ),
        cost_estimate=pl.CostEstimate(flops=0, bytes_accessed=100 << 20, transcendentals=0),
    )(key_states, value_states)


def local(queries, key_states, value_states, outputs, out_grad, doc_of_tile, tile_position):
    rows = queries.shape[0]
    kv_heads = key_states.shape[1] // HD
    head_count = lax.axis_size("head")
    ctx_count = lax.axis_size("ctx")
    ctx_index = lax.axis_index("ctx")
    split = kv_heads * head_count
    team = kv_heads
    near = [[b * team + s for s in range(team)] for b in range(ctx_count // team)]
    far = [[b * team + s for b in range(ctx_count // team)] for s in range(team)]

    def swap(value, split_axis, concat_axis):
        if head_count > 1:
            return lax.all_to_all(value, "head", split_axis, concat_axis, tiled=True)
        return lax.all_to_all(
            value, "ctx", split_axis, concat_axis, axis_index_groups=near, tiled=True
        )

    heads = queries.shape[1] // split // HD
    products = out_grad.astype(jnp.float32) * outputs.astype(jnp.float32)
    delta = jnp.sum(products.reshape(rows, split * heads, HD), axis=-1)
    if head_count == 1:
        kv_all = gather_head(key_states, value_states, ctx_count // team, team)
    else:
        kv = jnp.concatenate([key_states, value_states], axis=1)
        kv_all = lax.all_gather(kv, "ctx", axis=0, tiled=True, axis_index_groups=far)
    qd = jnp.concatenate(
        [
            queries.reshape(rows, split, heads * HD),
            out_grad.reshape(rows, split, heads * HD),
        ],
        axis=2,
    ).reshape(rows, split * 2 * heads * HD)
    qd = swap(qd, 1, 0)
    delta = swap(delta, 1, 0)
    many = qd.shape[0]
    tiles = many // TILE
    delta = jnp.transpose(delta.reshape(tiles, TILE, heads), (0, 2, 1)).reshape(
        tiles, 1, heads * TILE
    )
    count = tile_position.shape[0]
    order = jnp.arange(count, dtype=jnp.int32)
    inverse = jnp.sum(
        jnp.where(tile_position[None, :] == order[:, None], order[None, :], 0), axis=1
    ).astype(jnp.int32)
    places = lax.dynamic_slice_in_dim(tile_position, (ctx_index // team) * tiles, tiles)
    starts = jnp.sum(
        (doc_of_tile[None, :] < doc_of_tile[places][:, None]).astype(jnp.int32), axis=1
    ).astype(jnp.int32)
    dq, dkv = attention_backward(places, starts, inverse, qd, delta, kv_all)
    parts = ctx_count // team
    if head_count == 1:
        blocks = dq.reshape(team, rows, -1)
        me = ctx_index & (team - 1)
        home = jnp.zeros_like(blocks)
        for shift in range(team):
            piece = lax.dynamic_index_in_dim(blocks, me ^ shift, 0)
            if shift:
                pairs = [(i, i ^ shift) for i in range(ctx_count)]
                piece = lax.ppermute(piece, "ctx", pairs)
            home = lax.dynamic_update_slice_in_dim(home, piece, me ^ shift, 0)
        dq_home = jnp.transpose(home, (1, 0, 2)).reshape(rows, -1)
    dkv = lax.all_to_all(dkv, "ctx", 0, 0, axis_index_groups=far, tiled=True)
    dkv = jnp.sum(dkv.reshape(parts, -1, 2 * HD).astype(jnp.float32), axis=0).astype(jnp.bfloat16)
    if head_count == 1:
        dkv = swap(dkv, 0, 1)
        dq = dq_home
    dkv = dkv.reshape(dkv.shape[0], kv_heads, 2, HD)
    width = kv_heads * HD
    return (
        dq,
        dkv[:, :, 0].reshape(-1, width),
        dkv[:, :, 1].reshape(-1, width),
    )


def solution(mesh):
    placed = (
        P(("ctx", "head"), None),
        P("ctx", "head"),
        P("ctx", "head"),
        P(("ctx", "head"), None),
        P(("ctx", "head"), None),
        P(),
        P(),
    )
    return jax.shard_map(
        local,
        mesh=mesh,
        in_specs=placed,
        out_specs=(P("ctx", "head"), P("ctx", "head"), P("ctx", "head")),
        check_vma=False,
    )
```

```python
import functools

import jax
import jax.numpy as jnp
from jax import lax
from jax.experimental import pallas as pl
from jax.experimental.pallas import tpu as pltpu
from jax.sharding import PartitionSpec as P

HD = 128
TILE = 128
SPAN = 2
LOW = -1e30


def kernel(
    heads,
    tiles,
    place_ref,
    place_start_ref,
    inverse_ref,
    qd_ref,
    delta_ref,
    kv_ref,
    dq_ref,
    dkv_ref,
    q_rows,
    q_cols,
    g_rows,
    g_cols,
    score_buf,
    dq_acc,
    dkv_acc,
):
    width = heads * HD
    scale = HD ** (-0.5)
    keys = SPAN * TILE
    dkv_acc[...] = jnp.zeros_like(dkv_acc)
    row_id = lax.broadcasted_iota(jnp.int32, (keys, width), 0)
    col_id = lax.broadcasted_iota(jnp.int32, (keys, width), 1) & (TILE - 1)
    gap = row_id - col_id

    def spots(last):
        found = []
        for offset in range(SPAN):
            where = jnp.maximum(last - (SPAN - 1) + offset, 0)
            found.append(pl.multiple_of(inverse_ref[where] * TILE, TILE))
        return found

    def block(last, begin):
        return jnp.concatenate(
            [kv_ref[pl.ds(spot, TILE), begin : begin + HD] for spot in spots(last)], axis=0
        )

    @pl.loop(0, tiles)
    def _(tile):
        first_row = pl.multiple_of(tile * TILE, TILE)
        place = place_ref[tile]
        start = place_start_ref[tile]
        chunks = (place - start + SPAN) // SPAN
        for h in range(heads):
            lanes = slice(h * HD, (h + 1) * HD)
            q_block = qd_ref[pl.ds(first_row, TILE), h * HD : (h + 1) * HD]
            g_block = qd_ref[pl.ds(first_row, TILE), width + h * HD : width + (h + 1) * HD]
            q_rows[lanes, :] = q_block
            g_rows[lanes, :] = g_block
            q_cols[:, lanes] = q_block.T
            g_cols[:, lanes] = g_block.T

        def totals(step, state):
            top, total = state
            last = place - SPAN * step
            scores = (
                jnp.dot(block(last, 0), q_cols[...], preferred_element_type=jnp.float32) * scale
            )
            first_key = (last - (SPAN - 1)) * TILE
            visible = (gap <= place * TILE - first_key) & (row_id >= start * TILE - first_key)
            scores = jnp.where(visible, scores, LOW)
            score_buf[step] = scores
            new_top = jnp.maximum(top, jnp.max(scores, axis=0, keepdims=True))
            total = total * jnp.exp(top - new_top) + jnp.sum(
                jnp.exp(scores - new_top), axis=0, keepdims=True
            )
            return new_top, total

        top, total = lax.fori_loop(
            0,
            chunks,
            totals,
            (jnp.full((1, width), LOW, jnp.float32), jnp.zeros((1, width), jnp.float32)),
        )
        log_total = top + jnp.log(total)
        delta = delta_ref[tile]
        dq_acc[...] = jnp.zeros_like(dq_acc)

        @pl.loop(0, chunks)
        def _(step):
            last = place - SPAN * step
            k_block = block(last, 0)
            probs = jnp.exp(score_buf[step] - log_total)
            grad_probs = jnp.dot(
                block(last, HD), g_cols[...], preferred_element_type=jnp.float32
            )
            low = probs.astype(jnp.bfloat16)
            grad_scores = (probs * (grad_probs - delta) * scale).astype(jnp.bfloat16)
            dv = jnp.dot(low, g_rows[...], preferred_element_type=jnp.float32)
            dk = jnp.dot(grad_scores, q_rows[...], preferred_element_type=jnp.float32)
            dq_acc[...] += lax.dot_general(
                k_block,
                grad_scores,
                (((0,), (0,)), ((), ())),
                preferred_element_type=jnp.float32,
            )
            for offset, spot in enumerate(spots(last)):
                rows = slice(offset * TILE, (offset + 1) * TILE)
                dkv_acc[pl.ds(spot, TILE), 0:HD] += dk[rows]
                dkv_acc[pl.ds(spot, TILE), HD : 2 * HD] += dv[rows]

        for h in range(heads):
            lanes = slice(h * HD, (h + 1) * HD)
            dq_ref[pl.ds(first_row, TILE), lanes] = dq_acc[:, lanes].T.astype(jnp.bfloat16)

    dkv_ref[...] = dkv_acc[...].astype(jnp.bfloat16)


def attention_backward(places, starts, inverse, qd, delta, kv):
    rows, both = qd.shape
    width = both // 2
    heads = width // HD
    tokens = kv.shape[0]
    tiles = rows // TILE
    steps = tokens // TILE // SPAN
    smem = pl.BlockSpec(memory_space=pltpu.SMEM)
    vmem = pl.BlockSpec(memory_space=pltpu.VMEM)
    return pl.pallas_call(
        functools.partial(kernel, heads, tiles),
        out_shape=(
            jax.ShapeDtypeStruct((rows, width), jnp.bfloat16),
            jax.ShapeDtypeStruct((tokens, 2 * HD), jnp.bfloat16),
        ),
        in_specs=[smem, smem, smem, vmem, vmem, vmem],
        out_specs=(vmem, vmem),
        scratch_shapes=[
            pltpu.VMEM((width, HD), jnp.bfloat16),
            pltpu.VMEM((HD, width), jnp.bfloat16),
            pltpu.VMEM((width, HD), jnp.bfloat16),
            pltpu.VMEM((HD, width), jnp.bfloat16),
            pltpu.VMEM((steps // 2 + 1, SPAN * TILE, width), jnp.float32),
            pltpu.VMEM((HD, width), jnp.float32),
            pltpu.VMEM((tokens, 2 * HD), jnp.float32),
        ],
        compiler_params=pltpu.CompilerParams(vmem_limit_bytes=48 * 1024 * 1024),
        cost_estimate=pl.CostEstimate(
            flops=rows * width * tokens * 3, bytes_accessed=12 << 20, transcendentals=0
        ),
    )(places, starts, inverse, qd, delta, kv)


def gather_kernel(parts, team, k_ref, v_ref, out_ref, near_send, near_recv, far_send, far_recv):
    me = lax.axis_index("ctx")
    other = lax.axis_index("head")
    mine = me % team
    block = me // team
    half = parts // 2
    side = block % 2
    turn = (1 - side) * (block // 2) + side * (parts - 1 - block // 2)
    rows = k_ref.shape[0]

    def block_of(place):
        place = (place + parts) % parts
        upper = place // half
        return (1 - upper) * 2 * place + upper * (2 * (parts - 1 - place) + 1)

    right = block_of(turn + 1) * team + mine
    left = block_of(turn - 1) * team + mine
    friends = [block * team + (mine + shift) % team for shift in range(1, team)]
    barrier = pltpu.get_barrier_semaphore()
    for device in [left, right] + friends:
        pl.semaphore_signal(
            barrier, inc=1, device_id=(device, other), device_id_type=pl.DeviceIdType.MESH
        )
    pl.semaphore_wait(barrier, team + 1)
    home = pl.ds(pl.multiple_of(me * rows, TILE), rows)
    copies = []
    for which, ref in enumerate((k_ref, v_ref)):
        lanes = slice(which * HD, (which + 1) * HD)
        for shift in range(1, team):
            source = pl.ds(pl.multiple_of((mine + shift) % team * HD, HD), HD)
            copy = pltpu.make_async_remote_copy(
                src_ref=ref.at[:, source],
                dst_ref=out_ref.at[home, lanes],
                send_sem=near_send.at[which, shift - 1],
                recv_sem=near_recv.at[which, shift - 1],
                device_id=(friends[shift - 1], other),
                device_id_type=pl.DeviceIdType.MESH,
            )
            copy.start()
            copies.append(copy)
    for which, ref in enumerate((k_ref, v_ref)):
        own = pl.ds(pl.multiple_of(mine * HD, HD), HD)
        out_ref[home, which * HD : (which + 1) * HD] = ref[:, own]
    for copy in copies:
        copy.wait_recv()
    span = team * rows
    for step in range(half):
        moves = [(turn - step, right, 0)]
        if step < half - 1:
            moves.append((turn + step, left, 1))
        now = []
        for place, device, way in moves:
            area = pl.ds(pl.multiple_of(block_of(place) * span, TILE), span)
            copy = pltpu.make_async_remote_copy(
                src_ref=out_ref.at[area],
                dst_ref=out_ref.at[area],
                send_sem=far_send.at[way, step],
                recv_sem=far_recv.at[way, step],
                device_id=(device, other),
                device_id_type=pl.DeviceIdType.MESH,
            )
            copy.start()
            now.append(copy)
            copies.append(copy)
        for copy in now:
            copy.wait_recv()
    for copy in copies:
        copy.wait_send()


def gather_head(key_states, value_states, parts, team):
    rows = key_states.shape[0]
    vmem = pl.BlockSpec(memory_space=pltpu.VMEM)
    return pl.pallas_call(
        functools.partial(gather_kernel, parts, team),
        out_shape=jax.ShapeDtypeStruct((parts * team * rows, 2 * HD), jnp.bfloat16),
        in_specs=[vmem, vmem],
        out_specs=vmem,
        scratch_shapes=[
            pltpu.SemaphoreType.DMA((2, team - 1)),
            pltpu.SemaphoreType.DMA((2, team - 1)),
            pltpu.SemaphoreType.DMA((2, parts // 2)),
            pltpu.SemaphoreType.DMA((2, parts // 2)),
        ],
        compiler_params=pltpu.CompilerParams(
            collective_id=0, has_side_effects=True, vmem_limit_bytes=16 * 1024 * 1024
        ),
        cost_estimate=pl.CostEstimate(flops=0, bytes_accessed=100 << 20, transcendentals=0),
    )(key_states, value_states)


def local(queries, key_states, value_states, outputs, out_grad, doc_of_tile, tile_position):
    rows = queries.shape[0]
    kv_heads = key_states.shape[1] // HD
    head_count = lax.axis_size("head")
    ctx_count = lax.axis_size("ctx")
    ctx_index = lax.axis_index("ctx")
    split = kv_heads * head_count
    team = kv_heads
    near = [[b * team + s for s in range(team)] for b in range(ctx_count // team)]
    far = [[b * team + s for b in range(ctx_count // team)] for s in range(team)]

    def swap(value, split_axis, concat_axis):
        if head_count > 1:
            return lax.all_to_all(value, "head", split_axis, concat_axis, tiled=True)
        return lax.all_to_all(
            value, "ctx", split_axis, concat_axis, axis_index_groups=near, tiled=True
        )

    heads = queries.shape[1] // split // HD
    products = out_grad.astype(jnp.float32) * outputs.astype(jnp.float32)
    delta = jnp.sum(products.reshape(rows, split * heads, HD), axis=-1)
    if head_count == 1:
        kv_all = gather_head(key_states, value_states, ctx_count // team, team)
    else:
        kv = jnp.concatenate([key_states, value_states], axis=1)
        kv_all = lax.all_gather(kv, "ctx", axis=0, tiled=True, axis_index_groups=far)
    qd = jnp.concatenate(
        [
            queries.reshape(rows, split, heads * HD),
            out_grad.reshape(rows, split, heads * HD),
        ],
        axis=2,
    ).reshape(rows, split * 2 * heads * HD)
    qd = swap(qd, 1, 0)
    delta = swap(delta, 1, 0)
    many = qd.shape[0]
    tiles = many // TILE
    delta = jnp.transpose(delta.reshape(tiles, TILE, heads), (0, 2, 1)).reshape(
        tiles, 1, heads * TILE
    )
    count = tile_position.shape[0]
    order = jnp.arange(count, dtype=jnp.int32)
    inverse = jnp.sum(
        jnp.where(tile_position[None, :] == order[:, None], order[None, :], 0), axis=1
    ).astype(jnp.int32)
    places = lax.dynamic_slice_in_dim(tile_position, (ctx_index // team) * tiles, tiles)
    starts = jnp.sum(
        (doc_of_tile[None, :] < doc_of_tile[places][:, None]).astype(jnp.int32), axis=1
    ).astype(jnp.int32)
    dq, dkv = attention_backward(places, starts, inverse, qd, delta, kv_all)
    parts = ctx_count // team
    if head_count == 1:
        blocks = dq.reshape(team, rows, -1)
        me = ctx_index & (team - 1)
        pieces = []
        for shift in range(team):
            piece = lax.dynamic_index_in_dim(blocks, me ^ shift, 0)
            if shift:
                pairs = [(i, i ^ shift) for i in range(ctx_count)]
                piece = lax.ppermute(piece, "ctx", pairs)
            pieces.append(piece[0])
        columns = []
        for head in range(team):
            chosen = pieces[0]
            for shift in range(1, team):
                chosen = jnp.where((me ^ shift) == head, pieces[shift], chosen)
            columns.append(chosen)
        dq_home = jnp.concatenate(columns, axis=1)
    dkv = lax.all_to_all(dkv, "ctx", 0, 0, axis_index_groups=far, tiled=True)
    dkv = jnp.sum(dkv.reshape(parts, -1, 2 * HD).astype(jnp.float32), axis=0).astype(jnp.bfloat16)
    if head_count == 1:
        dkv = swap(dkv, 0, 1)
        dq = dq_home
    dkv = dkv.reshape(dkv.shape[0], kv_heads, 2, HD)
    width = kv_heads * HD
    return (
        dq,
        dkv[:, :, 0].reshape(-1, width),
        dkv[:, :, 1].reshape(-1, width),
    )


def solution(mesh):
    placed = (
        P(("ctx", "head"), None),
        P("ctx", "head"),
        P("ctx", "head"),
        P(("ctx", "head"), None),
        P(("ctx", "head"), None),
        P(),
        P(),
    )
    return jax.shard_map(
        local,
        mesh=mesh,
        in_specs=placed,
        out_specs=(P("ctx", "head"), P("ctx", "head"), P("ctx", "head")),
        check_vma=False,
    )
```
